128 devices in a mesh: img: 16 (over y_hi, z, core), head: 8 (over x, y_lo).
Axes of the slice: x: 4, y: 4 (y_hi: 2, y_lo: 2; y = y_hi * 2 + y_lo), z: 4, core: 2. Of those that a mesh axis runs over, the one named last changes fastest.
Arguments:
- hidden: bfloat16 [3, 32, 8192], P(None, None, ('img', 'head')), may hold values from -6 to 6
- vision: bfloat16 [16, 4, 1600, 8192], P('img', None, 'head'), may hold values from -6 to 6
- image_ids: int32 [32], replicated, may hold values from 0 to 15, as said below
- tile_counts: int32 [16], replicated, may hold values from 1 to 4
- q_weight: bfloat16 [8192, 8192], P(('img', 'head')), may hold values from -0.0625 to 0.0625
- q_gain: float32 [8192], replicated, may hold values from 0.5 to 50, as said below
- k_weight: bfloat16 [8192, 1024], P('img'), may hold values from -0.0625 to 0.0625
- v_weight: bfloat16 [8192, 1024], P('img'), may hold values from -0.0625 to 0.0625
- o_weight: bfloat16 [8192, 8192], P('head', 'img'), may hold values from -0.0625 to 0.0625
Outputs:
- layer_out: float32 [3, 32, 8192], P(None, 'head', 'img')
The draws below stay inside these ranges and needn't reach their ends.
Inputs may be any that keep to these rules, and one draw needn't show every extreme that they name: `image_ids`: each image is named by exactly two requests. `q_gain`: positive.
All inputs are finite; a program needn't handle non-finite values.
Results may differ from the reference program's by a relative error of at most 0.009.
The reference program's roundings to bfloat16 on the way (of `queries`, `key_heads`, `value_heads`, `probs` and `attention`) count: a program that leaves them out, or rounds other values in their place, can miss the bound.
Values may be sent and summed in bfloat16 or wider, within the bound.
No kernel may reach another device: no remote copies, remote signals or barrier semaphores. Data moves between devices by JAX's collectives and lax.ppermute only.
A program may use at most 128 MiB of HBM per device.

```python
import math
import jax
import jax.numpy as jnp
from jax import lax

D = 8192
HEADS = 64
KVH = 8
HD = 128
TILES = 4
VTOK = 1600
STEPS = 3
IMAGES = 16
REQUESTS = 32


def draw_image_ids(key, part):
    key = jax.random.fold_in(key, 3)
    return (jax.random.permutation(key, REQUESTS) // 2).astype(jnp.int32)


def draw_q_gain(key, part):
    key = jax.random.fold_in(key, 7)
    key_head, key_dim = jax.random.split(key, 2)
    per_dim = jax.random.uniform(key_dim, (HEADS * HD,), jnp.float32, 0.8, 1.2)
    head_scale = jnp.exp(jax.random.uniform(key_head, (HEADS,), jnp.float32, math.log(0.7), math.log(3.0)))
    return (jnp.repeat(head_scale, HD) * per_dim).astype(jnp.float32)


def with_ends(entries, rng, low, high):
    place = [jax.random.randint(jax.random.fold_in(rng, axis), (), 0, length) for axis, length in enumerate(entries.shape)]
    widest = entries.shape.index(max(entries.shape))
    neighbour = place[:widest] + [(place[widest] + 1) % entries.shape[widest]] + place[widest + 1:]
    return entries.at[tuple(place)].set(low).at[tuple(neighbour)].set(high)


def block_scale(rng, extent, cuts, low, high):
    level = 1.0
    for axis_at, parts in cuts:
        draws = jax.random.uniform(jax.random.fold_in(jax.random.fold_in(rng, 6), axis_at), (parts,), jnp.float32, low / len(cuts), high / len(cuts))
        level = level * jnp.repeat(jnp.exp(draws), extent[axis_at] // parts).reshape((-1,) + (1,) * (len(extent) - 1 - axis_at))
    return level


def scatter_about(stream_key, shape, deviation, reach, pieces=(), held_as=jnp.bfloat16):
    entries = jax.random.normal(stream_key, shape, jnp.float32) * deviation
    if len(pieces) > 0:
        entries = block_scale(stream_key, shape, pieces, -0.22, 0.18) * entries
    return jnp.clip(entries, min=-reach, max=reach).astype(held_as)


def setup_inputs(seed: int = 0) -> dict:
    key_of = jax.random.split(jax.random.key(seed), 10)
    hidden = scatter_about(key_of[0], (STEPS, REQUESTS, D), 1.0, 6.0, ((2, 128),))
    vision = scatter_about(key_of[1], (IMAGES, TILES, VTOK, D), 1.0, 6.0, ((0, 16), (2, 8)))
    image_ids = draw_image_ids(jax.random.fold_in(key_of[9], 71), 0)
    tile_counts = with_ends(jax.random.randint(key_of[3], (IMAGES,), 1, TILES + 1), jax.random.fold_in(key_of[3], 1), 1, TILES).astype(jnp.int32)
    q_weight = scatter_about(key_of[4], (D, HEADS * HD), D ** -0.5, 0.0625, ((0, 128),))
    q_gain = draw_q_gain(jax.random.fold_in(key_of[9], 71), 0)
    k_weight = scatter_about(key_of[6], (D, KVH * HD), D ** -0.5, 0.0625, ((0, 16),))
    v_weight = scatter_about(key_of[7], (D, KVH * HD), D ** -0.5, 0.0625, ((0, 16),))
    o_weight = scatter_about(key_of[8], (HEADS * HD, D), (HEADS * HD) ** -0.5, 0.0625, ((0, 8), (1, 16)))
    return {"hidden": hidden, "vision": vision, "image_ids": image_ids, "tile_counts": tile_counts, "q_weight": q_weight, "q_gain": q_gain, "k_weight": k_weight, "v_weight": v_weight, "o_weight": o_weight}


EPS = 1e-05

def normalize(vectors):
    return vectors * lax.rsqrt(lax.optimization_barrier(jnp.mean(vectors * vectors, axis=-1, keepdims=True)) + EPS)

def reference(hidden, vision, image_ids, tile_counts, q_weight, q_gain, k_weight, v_weight, o_weight):
    per_group = HEADS // KVH
    query_raw = jnp.dot(hidden.reshape(STEPS * REQUESTS, D), q_weight, preferred_element_type=jnp.float32)
    query_raw = query_raw.reshape(STEPS, REQUESTS, HEADS, HD)
    queries = (normalize(query_raw) * q_gain.reshape(HEADS, HD) * HD ** (-0.5)).astype(jnp.bfloat16)
    tile_of = jnp.repeat(jnp.arange(TILES, dtype=jnp.int32), VTOK)

    def one_image(image_no):
        image_no = image_no.astype(jnp.int32)
        features = lax.dynamic_index_in_dim(vision, image_no, 0, keepdims=False).reshape(TILES * VTOK, D)
        key_heads = jnp.dot(features, k_weight, preferred_element_type=jnp.float32).reshape(TILES * VTOK, KVH, HD)
        key_heads = normalize(key_heads).astype(jnp.bfloat16)
        value_heads = jnp.dot(features, v_weight, preferred_element_type=jnp.float32).astype(jnp.bfloat16)
        value_heads = value_heads.reshape(TILES * VTOK, KVH, HD)
        tile_limit = lax.dynamic_index_in_dim(tile_counts, image_no, 0, keepdims=False)
        usable = tile_of < tile_limit
        owner_rows = jnp.nonzero(image_ids == image_no, size=2)[0].astype(jnp.int32)
        picked = jnp.take(queries, owner_rows, axis=1).reshape(STEPS, 2, KVH, per_group, HD)
        scores = jnp.einsum('sokgd,tkd->sokgt', picked.astype(jnp.float32), key_heads.astype(jnp.float32))
        scores = jnp.where(usable, scores, -jnp.inf)
        row_max = lax.optimization_barrier(jnp.max(scores, axis=-1, keepdims=True))
        expo = jnp.exp(scores - row_max)
        row_total = lax.optimization_barrier(jnp.sum(expo, axis=-1))
        probs = lax.optimization_barrier(expo.astype(jnp.bfloat16)).astype(jnp.float32)
        weighted = jnp.einsum('sokgt,tkd->sokgd', probs, value_heads.astype(jnp.float32))
        result = (weighted / row_total[..., None]).astype(jnp.bfloat16)
        return result.reshape(STEPS, 2, HEADS * HD)
    per_image = lax.map(one_image, jnp.arange(IMAGES, dtype=jnp.int32))
    order = jnp.arange(REQUESTS, dtype=jnp.int32)
    same_image = image_ids[:, None] == image_ids[None, :]
    earlier = order[None, :] < order[:, None]
    occurrence = lax.optimization_barrier(jnp.sum(jnp.logical_and(same_image, earlier), axis=1)).astype(jnp.int32)
    attention = per_image[image_ids, :, occurrence]
    attention = jnp.transpose(attention, (1, 0, 2)).reshape(STEPS * REQUESTS, HEADS * HD)
    layer_out = jnp.dot(attention, o_weight, preferred_element_type=jnp.float32)
    return layer_out.reshape(STEPS, REQUESTS, D)
```

```python
import jax
import jax.numpy as jnp
from jax import lax
from jax.experimental import pallas as pl
from jax.experimental.pallas import tpu as pltpu
from jax.sharding import Mesh, PartitionSpec as P

HEADS = 64
KVH = 8
HD = 128
TILES = 4
STEPS = 3
EPS = 1e-05

AXES = ("yh", "z", "c", "x", "yl")
SIZES = (2, 4, 2, 4, 2)
F32 = jnp.float32
BF16 = jnp.bfloat16


def pair_a(v):
    return v ^ 1


def pair_b(v):
    return (((v + 1) ^ 1) - 1) % 4


def first(c, v):
    return pair_a(v) if c == 0 else pair_b(v)


def second(c, v):
    return pair_b(v) if c == 0 else pair_a(v)


def place(y, z, c, x):
    return ((((y // 2) * 4 + z) * 2 + c) * 4 + x) * 2 + (y % 2)


def table(move):
    return [
        (place(y, z, c, x), place(*move(y, z, c, x)))
        for y in range(4)
        for z in range(4)
        for c in range(2)
        for x in range(4)
    ]


CORE = table(lambda y, z, c, x: (y, z, 1 - c, x))
YC = table(lambda y, z, c, x: (pair_b(y), z, c, x))
YR = table(lambda y, z, c, x: (pair_a(y), z, c, x))
Z1 = table(lambda y, z, c, x: (y, first(c, z), c, x))
Z2 = table(lambda y, z, c, x: (y, second(c, z), c, x))
Y1 = table(lambda y, z, c, x: (first(c, y), z, c, x))
Y2 = table(lambda y, z, c, x: (second(c, y), z, c, x))
X1 = table(lambda y, z, c, x: (y, z, c, first(c, x)))
X2 = table(lambda y, z, c, x: (y, z, c, second(c, x)))


def send(value, moves):
    return lax.ppermute(value, AXES, moves)


def cat(*parts):
    return jnp.concatenate(parts, axis=0)


def mate(core, v, step):
    a = v ^ 1
    b = (((v + 1) ^ 1) + 3) % 4
    return jnp.where(core == step, a, b)


def take_rows(value, start, size):
    return lax.dynamic_slice_in_dim(value, start, size, 0)


def project(features, segments, index, size, total=None, norm=False, last=True):
    terms = len(segments[0][1])
    steps = sum(n for n, _ in segments)
    width = segments[0][1][0][0].shape[1]
    tokens = features[0].shape[0]
    arrays, in_specs, spans = [], [], []
    for t in range(terms):
        for value in features:
            arrays.append(value)
            in_specs.append(
                pl.BlockSpec((tokens, size), lambda i, idx, t=t: (0, idx[i * terms + t]))
            )
    start = 0
    for n, parts in segments:
        for value, offset, stride in parts:
            arrays.append(value)
            in_specs.append(
                pl.BlockSpec(
                    (size, width),
                    lambda i, idx, s=start, n=n, o=offset, m=stride: (
                        jnp.clip(i - s, 0, n - 1) * m + o,
                        0,
                    ),
                )
            )
        spans.append((start, start + n))
        start += n
    if total is not None:
        arrays.append(total)
        in_specs.append(pl.BlockSpec((2, tokens, width), lambda i, idx: (0, 0, 0)))

    def body(idx_ref, *refs):
        step = pl.program_id(0)
        left = refs[: 2 * terms]
        right = refs[2 * terms : 2 * terms + terms * len(segments)]
        out_ref, acc_ref = refs[-2:]

        @pl.when(step == 0)
        def _():
            if total is None:
                acc_ref[...] = jnp.zeros_like(acc_ref)
            else:
                acc_ref[...] = refs[-3][...]

        for k, (lo, hi) in enumerate(spans):

            @pl.when(jnp.logical_and(step >= lo, step < hi))
            def _(k=k):
                rows = [r[...] for r in right[k * terms : (k + 1) * terms]]
                rows = rows[0] if terms == 1 else jnp.concatenate(rows, axis=0)
                for i in range(2):
                    cols = [left[2 * t + i][...] for t in range(terms)]
                    cols = cols[0] if terms == 1 else jnp.concatenate(cols, axis=1)
                    acc_ref[i] += jnp.dot(cols, rows, preferred_element_type=F32)

        @pl.when(step == steps - 1)
        def _():
            if not last:
                out_ref[...] = acc_ref[...]
                return
            for i in range(2):
                for h in range(width // HD):
                    part = acc_ref[i, :, h * HD : (h + 1) * HD]
                    if norm:
                        mean = jnp.mean(part * part, axis=-1, keepdims=True)
                        part = part * lax.rsqrt(mean + EPS)
                    out_ref[i, :, h * HD : (h + 1) * HD] = part.astype(BF16)

    return pl.pallas_call(
        body,
        grid_spec=pltpu.PrefetchScalarGridSpec(
            num_scalar_prefetch=1,
            grid=(steps,),
            in_specs=in_specs,
            out_specs=pl.BlockSpec((2, tokens, width), lambda i, idx: (0, 0, 0)),
            scratch_shapes=[pltpu.VMEM((2, tokens, width), F32)],
        ),
        out_shape=jax.ShapeDtypeStruct((2, tokens, width), BF16 if last else F32),
        cost_estimate=pl.CostEstimate(
            flops=4 * tokens * size * terms * steps * width,
            bytes_accessed=4 * tokens * size * terms * steps,
            transcendentals=0,
        ),
        compiler_params=pltpu.CompilerParams(vmem_limit_bytes=52 * 1024 * 1024),
    )(jnp.stack(index).astype(jnp.int32), *arrays)


def project_keys(features, lower, upper, steps):
    tokens = features[0].shape[0]
    size, width = 512, 256
    count = len(steps)
    table = jnp.stack([jnp.stack([jnp.asarray(n, jnp.int32) for n in s]) for s in steps])
    span = count // 4

    def rows_at(column, busy):
        def at(i, idx):
            now = jnp.int32(0)
            for g in range(4):
                near = i - g * span
                use = jnp.clip(i, g * span, (g + 1) * span - 1)
                if g in busy:
                    now = jnp.where(
                        jnp.logical_or(near >= 0, g == min(busy)), idx[use * 3 + column], now
                    )
            return (now, 0)

        return at

    def body(idx_ref, m_ref, t_ref, l0, l1, u0, u1, out_ref, acc_ref):
        step = pl.program_id(0)

        @pl.when(step == 0)
        def _():
            acc_ref[...] = jnp.zeros_like(acc_ref)

        for g, (low, up) in enumerate(((l0, u0), (l0, u1), (l1, u0), (l1, u1))):

            @pl.when(step // span == g)
            def _(low=low, up=up):
                rows = jnp.concatenate([low[...], up[...]], axis=1)
                acc_ref[0] += jnp.dot(m_ref[...], rows, preferred_element_type=F32)
                acc_ref[1] += jnp.dot(t_ref[...], rows, preferred_element_type=F32)

        @pl.when(step == count - 1)
        def _():
            for i in range(2):
                for h in range(4):
                    part = acc_ref[i, :, h * HD : (h + 1) * HD]
                    mean = jnp.mean(part * part, axis=-1, keepdims=True)
                    out_ref[i, :, h * HD : (h + 1) * HD] = (part * lax.rsqrt(mean + EPS)).astype(BF16)

    column = pl.BlockSpec((tokens, size), lambda i, idx: (0, idx[i * 3]))
    shape = (2, tokens, 2 * width)
    return pl.pallas_call(
        body,
        grid_spec=pltpu.PrefetchScalarGridSpec(
            num_scalar_prefetch=1,
            grid=(count,),
            in_specs=[
                column,
                column,
                pl.BlockSpec((size, width), rows_at(1, (0, 1))),
                pl.BlockSpec((size, width), rows_at(1, (2, 3))),
                pl.BlockSpec((size, width), rows_at(2, (0, 2))),
                pl.BlockSpec((size, width), rows_at(2, (1, 3))),
            ],
            out_specs=pl.BlockSpec(shape, lambda i, idx: (0, 0, 0)),
            scratch_shapes=[pltpu.VMEM(shape, F32)],
        ),
        out_shape=jax.ShapeDtypeStruct(shape, BF16),
        cost_estimate=pl.CostEstimate(
            flops=8 * tokens * size * count * width,
            bytes_accessed=4 * tokens * size * count,
            transcendentals=0,
        ),
        compiler_params=pltpu.CompilerParams(vmem_limit_bytes=52 * 1024 * 1024),
    )(table.reshape(-1), *features, *lower, *upper)


def slots(core, v):
    one, two = mate(core, v, 0), mate(core, v, 1)
    return (v, one, two, mate(core, two, 0))


def after(value, *others):
    return lax.optimization_barrier((value,) + others)[0]


def per_device(
    hidden, vision, image_ids, tile_counts, q_weight, q_gain, k_weight, v_weight, o_weight
):
    pos = tuple(lax.axis_index(a) for a in AXES)
    yh, z, core, x, yl = pos
    zs, xs = slots(core, z), slots(core, x)
    ys = slots(core, yh * 2 + yl)
    requests = hidden.shape[1]
    order = jnp.arange(requests, dtype=jnp.int32)
    same_image = image_ids[:, None] == image_ids[None, :]
    earlier = order[None, :] < order[:, None]
    occurrence = jnp.sum(jnp.logical_and(same_image, earlier), axis=1)
    slot_of = 2 * image_ids + occurrence
    request_at = jnp.sum(jnp.where(slot_of[None, :] == order[:, None], order[None, :], 0), axis=1)

    def column_half(w, which, width):
        return lax.dynamic_slice_in_dim(w, which * width, width, 1)

    def leaving(one, two):
        zpairs = ((z, two), (one, zs[3]))
        places = [
            (h * 4 + zz) * 4 + k for zp in zpairs for h in (yh, 1 - yh) for zz in zp for k in range(4)
        ]
        rows = jnp.take(hidden, jnp.take(request_at, jnp.stack(places)), axis=1)
        return rows.transpose(1, 0, 2).reshape(96, 64)

    give = cat(column_half(k_weight, 1 - core, 512), column_half(v_weight, 1 - core, 512))
    got = send(give, CORE)
    others = leaving(zs[2], zs[1])
    q_give = jnp.dot(
        after(others, give), column_half(q_weight, 1 - core, 4096), preferred_element_type=F32
    )
    q_got = send(q_give, CORE)
    q_mine = jnp.dot(
        leaving(zs[1], zs[2]), column_half(q_weight, core, 4096), preferred_element_type=F32
    )
    mine = vision.reshape(800, 8192)
    got = after(got, q_give)
    k_mine, v_mine = column_half(k_weight, core, 512), column_half(v_weight, core, 512)
    k_theirs, v_theirs = got[:512], got[512:]
    a0 = jnp.where(core == yl, k_mine[:, :256], k_theirs[:, :256])
    b0 = cat(k_mine[:, 256:], k_theirs[:, 256:])
    c0 = jnp.where(core == x // 2, v_mine, v_theirs)
    c0 = take_rows(c0, (x % 2) * 256, 256)
    c1 = send(c0, YC)
    a1 = send(a0, Z1)
    b1 = send(after(b0, a0, c0), YC)
    theirs = send(after(mine, b0), CORE)
    a01 = cat(a0, after(a1, b0))
    a2 = send(a01, Z2)
    c01 = cat(c0, after(c1, a01))
    c2 = send(c01, Z1)
    a0123 = cat(a01, after(a2, c01))
    a4 = send(a0123, Y1)
    c12 = cat(c1, after(c2, a0123))
    d1 = send(c12, X1)
    c0123 = cat(c01, after(c2, c12))
    c3 = send(c0123, Z2)
    q1 = send(after(q_mine[48:], c0123) + q_got[48:], Z1)
    d12 = cat(c12, after(d1, c0123, theirs))
    d2 = send(d12, X2)
    b01 = cat(b0, after(b1, d12))
    b2 = send(b01, Z1)
    c3 = after(c3, b01)
    e1 = send(c3, X1)
    q2 = q_mine[:48] + q_got[:48] + after(q1, c3)
    q3 = send(q2[24:], YC)
    a01234 = cat(a0123, after(a4, q2))
    a5 = send(a01234, Y2)
    q4 = q2[:24] + after(q3, a01234)
    q5 = send(q4[12:], Z2)
    b0123 = cat(b01, after(b2, q4))
    b3 = send(b0123, Z2)
    q6 = q4[:12] + after(q5, b0123)
    q7 = send(q6, YR)
    features = (mine, theirs)

    def color(h, zz):
        return h * 4 + zz

    def both(zz):
        return [color(yh, zz), color(1 - yh, zz)]

    def quarters(places):
        return [p * 4 + xx for p in places for xx in xs]

    def shared(n, own, one, two):
        return (n, ((own, 0, 1), (one, 0, 1), (two, 0, 1), (two, n, 1)))

    halved = [(v_mine, 0, 1), (v_mine, 1, 1), (v_theirs, 0, 1), (v_theirs, 1, 1)]
    index = [(color(yh, z) * 2 + cc) * 2 + t for cc in (core, 1 - core) for t in range(2)]
    index += quarters([color(1 - yh, z)] + both(zs[1]))
    values = project(
        features,
        [(1, tuple(halved)), shared(3, c12, d1, after(d2, q6))],
        index,
        256,
        last=False,
    )
    q8 = q6 + after(q7, values)
    q9 = send(q8, X1)
    e12 = cat(c3, after(e1, q8))
    e2 = send(e12, X2)
    steps = []
    for ks in ((0, 1), (2, 3)):
        for js in ((0, 1), (2, 3)):
            for k in ks:
                for j in js:
                    h, cc = ys[k] // 2, ys[k] % 2
                    spot = (j % 2) * 4 + jnp.where(h == yh, 0, 2) + jnp.where(cc == core, 0, 1)
                    steps.append((color(h, zs[j]) * 2 + cc, (k % 2) * 4 + j, spot))
    keys = project_keys(features, (a01234, after(a5, e12)), (b0123, b3), steps)
    q10 = q8 + after(q9, keys)
    q11 = send(q10, X2)
    value_heads = project(
        features,
        [shared(4, c3, e1, e2)],
        quarters(both(zs[2]) + both(zs[3])),
        256,
        total=after(values, q10),
    )
    value = q10 + after(q11, value_heads)

    raw = value.reshape(4, STEPS, 32, HD)
    norm = raw * lax.rsqrt(jnp.mean(raw * raw, axis=-1, keepdims=True) + EPS)
    gain = lax.dynamic_slice_in_dim(q_gain.reshape(HEADS, HD), core * 32, 32, 0)
    queries = (norm * gain * HD ** (-0.5)).astype(BF16)
    queries = queries.reshape(2, 2 * STEPS, 4, 8, HD).transpose(0, 2, 1, 3, 4).reshape(2, 4, 48, HD)
    queries = jnp.where(core == 0, queries, queries[::-1])
    limits = lax.dynamic_slice_in_dim(tile_counts, (yh * 4 + z) * 2, 2)
    limits = jnp.where(core == 0, limits, limits[::-1])
    usable = (jnp.arange(800, dtype=jnp.int32) // 200)[None, :] < limits[:, None]

    keys = keys.reshape(2, 800, 4, HD)
    scores = jnp.einsum("ikrd,itkd->ikrt", queries, keys, preferred_element_type=F32)
    scores = jnp.where(usable[:, None, None, :], scores, -jnp.inf)
    peak = jnp.max(scores, axis=-1, keepdims=True)
    expo = jnp.exp(scores - peak)
    total = jnp.sum(expo, axis=-1, keepdims=True)
    probs = (expo / total).astype(BF16)
    weight = (peak + jnp.log(total))[..., 0]
    high = lax.reduce_precision(weight, 8, 7)
    middle = lax.reduce_precision(weight - high, 8, 7)
    low = lax.reduce_precision(weight - high - middle, 8, 7)
    weight = jnp.stack([high, middle, low], axis=-1)
    weight = jnp.pad(weight, ((0, 0),) * 3 + ((0, HD - 3),))
    value_heads = value_heads.reshape(2, 800, 4, HD)
    part = jnp.einsum("ikrt,itkd->ikrd", probs, value_heads, preferred_element_type=F32)
    part = jnp.concatenate([part, weight], axis=2).astype(BF16)
    part = jnp.where(core == 0, part, part[::-1]).transpose(1, 0, 2, 3)
    got = lax.all_to_all(cat(part, part), ("x", "yl"), 0, 0, tiled=True)
    got = got.astype(F32)
    weight = jnp.sum(got[:, :, 48:, :3], axis=-1, keepdims=True)
    weight = jnp.exp(weight - jnp.max(weight, axis=0, keepdims=True))
    weight = weight / jnp.sum(weight, axis=0, keepdims=True)
    attention = jnp.sum(got[:, :, :48] * weight, axis=0).astype(BF16)
    spread = jnp.broadcast_to(attention[None], (16,) + attention.shape)
    got = lax.all_to_all(spread, ("yh", "z", "c"), 0, 0, tiled=True)
    got = got.reshape((8, 2) + attention.shape)
    attention = jnp.where(x < 2, got[:, 0], got[:, 1])
    attention = attention.reshape(96, 1024)
    terms = jnp.dot(attention, o_weight, preferred_element_type=F32).reshape(32, STEPS, 512)
    terms = jnp.take(terms, slot_of, axis=0).reshape(8, 4, STEPS, 512)
    got = lax.all_to_all(terms, ("x", "yl"), 0, 0, tiled=True)
    return jnp.sum(got, axis=0).transpose(1, 0, 2)


def solution(mesh):
    inner = Mesh(mesh.devices.reshape(SIZES), AXES)
    img, head = ("yh", "z", "c"), ("x", "yl")
    placed = (
        P(None, None, img + head),
        P(img, None, head, None),
        P(),
        P(),
        P(img + head, None),
        P(),
        P(img, None),
        P(img, None),
        P(head, img),
    )
    return jax.shard_map(
        per_device, mesh=inner, in_specs=placed, out_specs=P(None, head, img), check_vma=False
    )
```

```python
import jax
import jax.numpy as jnp
from jax import lax
from jax.experimental import pallas as pl
from jax.experimental.pallas import tpu as pltpu
from jax.sharding import Mesh, PartitionSpec as P

HEADS = 64
KVH = 8
HD = 128
TILES = 4
STEPS = 3
EPS = 1e-05

AXES = ("yh", "z", "c", "x", "yl")
SIZES = (2, 4, 2, 4, 2)
F32 = jnp.float32
BF16 = jnp.bfloat16


def pair_a(v):
    return v ^ 1


def pair_b(v):
    return (((v + 1) ^ 1) - 1) % 4


def first(c, v):
    return pair_a(v) if c == 0 else pair_b(v)


def second(c, v):
    return pair_b(v) if c == 0 else pair_a(v)


def place(y, z, c, x):
    return ((((y // 2) * 4 + z) * 2 + c) * 4 + x) * 2 + (y % 2)


def table(move):
    return [
        (place(y, z, c, x), place(*move(y, z, c, x)))
        for y in range(4)
        for z in range(4)
        for c in range(2)
        for x in range(4)
    ]


CORE = table(lambda y, z, c, x: (y, z, 1 - c, x))
YC = table(lambda y, z, c, x: (pair_b(y), z, c, x))
YR = table(lambda y, z, c, x: (pair_a(y), z, c, x))
Z1 = table(lambda y, z, c, x: (y, first(c, z), c, x))
Z2 = table(lambda y, z, c, x: (y, second(c, z), c, x))
Y1 = table(lambda y, z, c, x: (first(c, y), z, c, x))
Y2 = table(lambda y, z, c, x: (second(c, y), z, c, x))
X1 = table(lambda y, z, c, x: (y, z, c, first(c, x)))
X2 = table(lambda y, z, c, x: (y, z, c, second(c, x)))


def send(value, moves):
    return lax.ppermute(value, AXES, moves)


def cat(*parts):
    return jnp.concatenate(parts, axis=0)


def mate(core, v, step):
    a = v ^ 1
    b = (((v + 1) ^ 1) + 3) % 4
    return jnp.where(core == step, a, b)


def take_rows(value, start, size):
    return lax.dynamic_slice_in_dim(value, start, size, 0)


def project(features, segments, index, size, total=None, norm=False, last=True):
    terms = len(segments[0][1])
    steps = sum(n for n, _ in segments)
    width = segments[0][1][0][0].shape[1]
    tokens = features[0].shape[0]
    arrays, in_specs, spans = [], [], []
    for t in range(terms):
        for value in features:
            arrays.append(value)
            in_specs.append(
                pl.BlockSpec((tokens, size), lambda i, idx, t=t: (0, idx[i * terms + t]))
            )
    start = 0
    for n, parts in segments:
        for value, offset, stride in parts:
            arrays.append(value)
            in_specs.append(
                pl.BlockSpec(
                    (size, width),
                    lambda i, idx, s=start, n=n, o=offset, m=stride: (
                        jnp.clip(i - s, 0, n - 1) * m + o,
                        0,
                    ),
                )
            )
        spans.append((start, start + n))
        start += n
    if total is not None:
        arrays.append(total)
        in_specs.append(pl.BlockSpec((2, tokens, width), lambda i, idx: (0, 0, 0)))

    def body(idx_ref, *refs):
        step = pl.program_id(0)
        left = refs[: 2 * terms]
        right = refs[2 * terms : 2 * terms + terms * len(segments)]
        out_ref, acc_ref = refs[-2:]

        @pl.when(step == 0)
        def _():
            if total is None:
                acc_ref[...] = jnp.zeros_like(acc_ref)
            else:
                acc_ref[...] = refs[-3][...]

        for k, (lo, hi) in enumerate(spans):

            @pl.when(jnp.logical_and(step >= lo, step < hi))
            def _(k=k):
                rows = [r[...] for r in right[k * terms : (k + 1) * terms]]
                rows = rows[0] if terms == 1 else jnp.concatenate(rows, axis=0)
                for i in range(2):
                    cols = [left[2 * t + i][...] for t in range(terms)]
                    cols = cols[0] if terms == 1 else jnp.concatenate(cols, axis=1)
                    acc_ref[i] += jnp.dot(cols, rows, preferred_element_type=F32)

        @pl.when(step == steps - 1)
        def _():
            if not last:
                out_ref[...] = acc_ref[...]
                return
            for i in range(2):
                for h in range(width // HD):
                    part = acc_ref[i, :, h * HD : (h + 1) * HD]
                    if norm:
                        mean = jnp.mean(part * part, axis=-1, keepdims=True)
                        part = part * lax.rsqrt(mean + EPS)
                    out_ref[i, :, h * HD : (h + 1) * HD] = part.astype(BF16)

    return pl.pallas_call(
        body,
        grid_spec=pltpu.PrefetchScalarGridSpec(
            num_scalar_prefetch=1,
            grid=(steps,),
            in_specs=in_specs,
            out_specs=pl.BlockSpec((2, tokens, width), lambda i, idx: (0, 0, 0)),
            scratch_shapes=[pltpu.VMEM((2, tokens, width), F32)],
        ),
        out_shape=jax.ShapeDtypeStruct((2, tokens, width), BF16 if last else F32),
        cost_estimate=pl.CostEstimate(
            flops=4 * tokens * size * terms * steps * width,
            bytes_accessed=4 * tokens * size * terms * steps,
            transcendentals=0,
        ),
        compiler_params=pltpu.CompilerParams(vmem_limit_bytes=52 * 1024 * 1024),
    )(jnp.stack(index).astype(jnp.int32), *arrays)


def project_keys(features, lower, upper, steps):
    tokens = features[0].shape[0]
    size, width, terms = 512, 256, 2
    count = len(steps) // terms
    table = jnp.stack([jnp.stack([jnp.asarray(n, jnp.int32) for n in s]) for s in steps])
    span = count // 4

    def rows_at(column, busy, t):
        def at(i, idx):
            now = jnp.int32(0)
            for g in busy:
                use = jnp.clip(i, g * span, (g + 1) * span - 1)
                spot = idx[(use * terms + t) * 3 + column]
                now = jnp.where(jnp.logical_or(i >= g * span, g == busy[0]), spot, now)
            return (now, 0)

        return at

    def body(idx_ref, *refs):
        step = pl.program_id(0)
        out_ref, acc_ref = refs[-2:]
        left, right = refs[: 2 * terms], refs[2 * terms : -2]

        @pl.when(step == 0)
        def _():
            acc_ref[...] = jnp.zeros_like(acc_ref)

        for g, (low, up) in enumerate(((0, 2), (0, 3), (1, 2), (1, 3))):

            @pl.when(step // span == g)
            def _(low=low, up=up):
                rows = jnp.concatenate(
                    [
                        jnp.concatenate([right[4 * t + low][...], right[4 * t + up][...]], axis=1)
                        for t in range(terms)
                    ],
                    axis=0,
                )
                for i in range(2):
                    cols = jnp.concatenate([left[2 * t + i][...] for t in range(terms)], axis=1)
                    acc_ref[i] += jnp.dot(cols, rows, preferred_element_type=F32)

        @pl.when(step == count - 1)
        def _():
            for i in range(2):
                for h in range(4):
                    part = acc_ref[i, :, h * HD : (h + 1) * HD]
                    mean = jnp.mean(part * part, axis=-1, keepdims=True)
                    out_ref[i, :, h * HD : (h + 1) * HD] = (part * lax.rsqrt(mean + EPS)).astype(BF16)

    arrays, in_specs = [], []
    for t in range(terms):
        arrays += features
        in_specs += [
            pl.BlockSpec((tokens, size), lambda i, idx, t=t: (0, idx[(i * terms + t) * 3]))
        ] * 2
    for t in range(terms):
        arrays += [*lower, *upper]
        for column, busy in ((1, (0, 1)), (1, (2, 3)), (2, (0, 2)), (2, (1, 3))):
            in_specs.append(pl.BlockSpec((size, width), rows_at(column, busy, t)))
    shape = (2, tokens, 2 * width)
    return pl.pallas_call(
        body,
        grid_spec=pltpu.PrefetchScalarGridSpec(
            num_scalar_prefetch=1,
            grid=(count,),
            in_specs=in_specs,
            out_specs=pl.BlockSpec(shape, lambda i, idx: (0, 0, 0)),
            scratch_shapes=[pltpu.VMEM(shape, F32)],
        ),
        out_shape=jax.ShapeDtypeStruct(shape, BF16),
        cost_estimate=pl.CostEstimate(
            flops=8 * tokens * size * terms * count * width,
            bytes_accessed=4 * tokens * size * terms * count,
            transcendentals=0,
        ),
        compiler_params=pltpu.CompilerParams(vmem_limit_bytes=52 * 1024 * 1024),
    )(table.reshape(-1), *arrays)


def slots(core, v):
    one, two = mate(core, v, 0), mate(core, v, 1)
    return (v, one, two, mate(core, two, 0))


def after(value, *others):
    return lax.optimization_barrier((value,) + others)[0]


def per_device(
    hidden, vision, image_ids, tile_counts, q_weight, q_gain, k_weight, v_weight, o_weight
):
    pos = tuple(lax.axis_index(a) for a in AXES)
    yh, z, core, x, yl = pos
    zs, xs = slots(core, z), slots(core, x)
    ys = slots(core, yh * 2 + yl)
    requests = hidden.shape[1]
    order = jnp.arange(requests, dtype=jnp.int32)
    same_image = image_ids[:, None] == image_ids[None, :]
    earlier = order[None, :] < order[:, None]
    occurrence = jnp.sum(jnp.logical_and(same_image, earlier), axis=1)
    slot_of = 2 * image_ids + occurrence
    request_at = jnp.sum(jnp.where(slot_of[None, :] == order[:, None], order[None, :], 0), axis=1)

    def column_half(w, which, width):
        return lax.dynamic_slice_in_dim(w, which * width, width, 1)

    def leaving(one, two):
        zpairs = ((z, two), (one, zs[3]))
        return [
            (h * 4 + zz) * 4 + k for zp in zpairs for h in (yh, 1 - yh) for zz in zp for k in range(4)
        ]

    give = cat(column_half(k_weight, 1 - core, 512), column_half(v_weight, 1 - core, 512))
    got = send(give, CORE)
    places = jnp.stack(leaving(zs[2], zs[1]) + leaving(zs[1], zs[2]))
    rows = jnp.take(hidden, jnp.take(request_at, places), axis=1)
    rows = after(rows.transpose(1, 0, 2).reshape(192, 64), give)
    q_give = jnp.dot(
        rows[:96], column_half(q_weight, 1 - core, 4096), preferred_element_type=F32
    )
    q_got = send(q_give, CORE)
    mine = vision.reshape(800, 8192)
    got = after(got, q_give)
    k_mine, v_mine = column_half(k_weight, core, 512), column_half(v_weight, core, 512)
    k_theirs, v_theirs = got[:512], got[512:]
    a0 = jnp.where(core == yl, k_mine[:, :256], k_theirs[:, :256])
    b0 = cat(k_mine[:, 256:], k_theirs[:, 256:])
    c0 = jnp.where(core == x // 2, v_mine, v_theirs)
    c0 = take_rows(c0, (x % 2) * 256, 256)
    c1 = send(c0, YC)
    a1 = send(a0, Z1)
    b1 = send(after(b0, a0, c0), YC)
    theirs = send(after(mine, b0, a0, c0), CORE)
    q_mine = jnp.dot(
        after(rows, a0, c0)[96:], column_half(q_weight, core, 4096), preferred_element_type=F32
    )
    a01 = cat(a0, after(a1, b0))
    a2 = send(a01, Z2)
    c01 = cat(c0, after(c1, a01))
    c2 = send(c01, Z1)
    a0123 = cat(a01, after(a2, c01))
    a4 = send(a0123, Y1)
    c12 = cat(c1, after(c2, a0123))
    d1 = send(c12, X1)
    c0123 = cat(c01, after(c2, c12))
    c3 = send(c0123, Z2)
    q1 = send(after(q_mine[48:], c0123) + q_got[48:], Z1)
    d12 = cat(c12, after(d1, c0123, theirs))
    d2 = send(d12, X2)
    b01 = cat(b0, after(b1, d12))
    b2 = send(b01, Z1)
    c3 = after(c3, b01)
    e1 = send(c3, X1)
    q2 = q_mine[:48] + q_got[:48] + after(q1, c3)
    q3 = send(q2[24:], YC)
    a01234 = cat(a0123, after(a4, q2))
    a5 = send(a01234, Y2)
    q4 = q2[:24] + after(q3, a01234)
    q5 = send(q4[12:], Z2)
    b0123 = cat(b01, after(b2, q4))
    b3 = send(b0123, Z2)
    q6 = q4[:12] + after(q5, b0123)
    q7 = send(q6, YR)
    features = (mine, theirs)

    def color(h, zz):
        return h * 4 + zz

    def both(zz):
        return [color(yh, zz), color(1 - yh, zz)]

    def quarters(places):
        return [p * 4 + xx for p in places for xx in xs]

    def shared(n, own, one, two):
        return (n, ((own, 0, 1), (one, 0, 1), (two, 0, 1), (two, n, 1)))

    halved = [(v_mine, 0, 1), (v_mine, 1, 1), (v_theirs, 0, 1), (v_theirs, 1, 1)]
    index = [(color(yh, z) * 2 + cc) * 2 + t for cc in (core, 1 - core) for t in range(2)]
    index += quarters([color(1 - yh, z)] + both(zs[1]))
    values = project(
        features,
        [(1, tuple(halved)), shared(3, c12, d1, after(d2, q6))],
        index,
        256,
        last=False,
    )
    q8 = q6 + after(q7, values)
    q9 = send(q8, X1)
    e12 = cat(c3, after(e1, q8))
    e2 = send(e12, X2)
    steps = []
    for ks in ((0, 1), (2, 3)):
        for js in ((0, 1), (2, 3)):
            for k in ks:
                for j in js:
                    h, cc = ys[k] // 2, ys[k] % 2
                    spot = (j % 2) * 4 + jnp.where(h == yh, 0, 2) + jnp.where(cc == core, 0, 1)
                    steps.append((color(h, zs[j]) * 2 + cc, (k % 2) * 4 + j, spot))
    keys = project_keys(features, (a01234, after(a5, e12)), (b0123, b3), steps)
    q10 = q8 + after(q9, keys)
    q11 = send(q10, X2)
    value_heads = project(
        features,
        [shared(4, c3, e1, e2)],
        quarters(both(zs[2]) + both(zs[3])),
        256,
        total=after(values, q10),
    )
    value = q10 + after(q11, value_heads)

    raw = value.reshape(4, STEPS, 32, HD)
    norm = raw * lax.rsqrt(jnp.mean(raw * raw, axis=-1, keepdims=True) + EPS)
    gain = lax.dynamic_slice_in_dim(q_gain.reshape(HEADS, HD), core * 32, 32, 0)
    queries = (norm * gain * HD ** (-0.5)).astype(BF16)
    queries = queries.reshape(2, 2 * STEPS, 4, 8, HD).transpose(0, 2, 1, 3, 4).reshape(2, 4, 48, HD)
    queries = jnp.where(core == 0, queries, queries[::-1])
    limits = lax.dynamic_slice_in_dim(tile_counts, (yh * 4 + z) * 2, 2)
    limits = jnp.where(core == 0, limits, limits[::-1])
    usable = (jnp.arange(800, dtype=jnp.int32) // 200)[None, :] < limits[:, None]

    keys = keys.reshape(2, 800, 4, HD)
    scores = jnp.einsum("ikrd,itkd->ikrt", queries, keys, preferred_element_type=F32)
    scores = jnp.where(usable[:, None, None, :], scores, -jnp.inf)
    peak = jnp.max(scores, axis=-1, keepdims=True)
    expo = jnp.exp(scores - peak)
    total = jnp.sum(expo, axis=-1, keepdims=True)
    probs = (expo / total).astype(BF16)
    weight = (peak + jnp.log(total))[..., 0]
    high = lax.reduce_precision(weight, 8, 7)
    middle = lax.reduce_precision(weight - high, 8, 7)
    low = lax.reduce_precision(weight - high - middle, 8, 7)
    weight = jnp.stack([high, middle, low], axis=-1)
    weight = jnp.pad(weight, ((0, 0),) * 3 + ((0, HD - 3),))
    value_heads = value_heads.reshape(2, 800, 4, HD)
    part = jnp.einsum("ikrt,itkd->ikrd", probs, value_heads, preferred_element_type=F32)
    part = jnp.concatenate([part, weight], axis=2).astype(BF16)
    part = jnp.where(core == 0, part, part[::-1]).transpose(1, 0, 2, 3)
    got = lax.all_to_all(cat(part, part), ("x", "yl"), 0, 0, tiled=True)
    got = got.astype(F32)
    weight = jnp.sum(got[:, :, 48:, :3], axis=-1, keepdims=True)
    weight = jnp.exp(weight - jnp.max(weight, axis=0, keepdims=True))
    weight = weight / jnp.sum(weight, axis=0, keepdims=True)
    attention = jnp.sum(got[:, :, :48] * weight, axis=0).astype(BF16)
    there = send(attention, CORE)
    attention = jnp.where((core == 0) == (x < 2), attention, there)
    spread = jnp.broadcast_to(attention[None], (8,) + attention.shape)
    attention = lax.all_to_all(spread, ("yh", "z"), 0, 0, tiled=True)
    attention = attention.reshape(96, 1024)
    terms = jnp.dot(attention, o_weight, preferred_element_type=F32).reshape(32, STEPS, 512)
    terms = jnp.take(terms, slot_of, axis=0).reshape(8, 4, STEPS, 512)
    got = lax.all_to_all(terms, ("x", "yl"), 0, 0, tiled=True)
    return jnp.sum(got, axis=0).transpose(1, 0, 2)


def solution(mesh):
    inner = Mesh(mesh.devices.reshape(SIZES), AXES)
    img, head = ("yh", "z", "c"), ("x", "yl")
    placed = (
        P(None, None, img + head),
        P(img, None, head, None),
        P(),
        P(),
        P(img + head, None),
        P(),
        P(img, None),
        P(img, None),
        P(head, img),
    )
    return jax.shard_map(
        per_device, mesh=inner, in_specs=placed, out_specs=P(None, head, img), check_vma=False
    )
```

```python
import jax
import jax.numpy as jnp
from jax import lax
from jax.experimental import pallas as pl
from jax.experimental.pallas import tpu as pltpu
from jax.sharding import Mesh, PartitionSpec as P

HEADS = 64
KVH = 8
HD = 128
TILES = 4
STEPS = 3
EPS = 1e-05

AXES = ("yh", "z", "c", "x", "yl")
SIZES = (2, 4, 2, 4, 2)
F32 = jnp.float32
BF16 = jnp.bfloat16


def pair_a(v):
    return v ^ 1


def pair_b(v):
    return (((v + 1) ^ 1) - 1) % 4


def first(c, v):
    return pair_a(v) if c == 0 else pair_b(v)


def second(c, v):
    return pair_b(v) if c == 0 else pair_a(v)


def place(y, z, c, x):
    return ((((y // 2) * 4 + z) * 2 + c) * 4 + x) * 2 + (y % 2)


def table(move):
    return [
        (place(y, z, c, x), place(*move(y, z, c, x)))
        for y in range(4)
        for z in range(4)
        for c in range(2)
        for x in range(4)
    ]


CORE = table(lambda y, z, c, x: (y, z, 1 - c, x))
YC = table(lambda y, z, c, x: (pair_b(y), z, c, x))
YR = table(lambda y, z, c, x: (pair_a(y), z, c, x))
Z1 = table(lambda y, z, c, x: (y, first(c, z), c, x))
Z2 = table(lambda y, z, c, x: (y, second(c, z), c, x))
Y1 = table(lambda y, z, c, x: (first(c, y), z, c, x))
Y2 = table(lambda y, z, c, x: (second(c, y), z, c, x))
X1 = table(lambda y, z, c, x: (y, z, c, first(c, x)))
X2 = table(lambda y, z, c, x: (y, z, c, second(c, x)))


def send(value, moves):
    return lax.ppermute(value, AXES, moves)


def cat(*parts):
    return jnp.concatenate(parts, axis=0)


def mate(core, v, step):
    a = v ^ 1
    b = (((v + 1) ^ 1) + 3) % 4
    return jnp.where(core == step, a, b)


def take_rows(value, start, size):
    return lax.dynamic_slice_in_dim(value, start, size, 0)


def project(features, segments, index, size, total=None, norm=False, last=True):
    terms = len(segments[0][1])
    steps = sum(n for n, _ in segments)
    width = segments[0][1][0][0].shape[1]
    tokens = features[0].shape[0]
    arrays, in_specs, spans = [], [], []
    for t in range(terms):
        for value in features:
            arrays.append(value)
            in_specs.append(
                pl.BlockSpec((tokens, size), lambda i, idx, t=t: (0, idx[i * terms + t]))
            )
    start = 0
    for n, parts in segments:
        for value, offset, stride in parts:
            arrays.append(value)
            in_specs.append(
                pl.BlockSpec(
                    (size, width),
                    lambda i, idx, s=start, n=n, o=offset, m=stride: (
                        jnp.clip(i - s, 0, n - 1) * m + o,
                        0,
                    ),
                )
            )
        spans.append((start, start + n))
        start += n
    if total is not None:
        arrays.append(total)
        in_specs.append(pl.BlockSpec((2, tokens, width), lambda i, idx: (0, 0, 0)))

    def body(idx_ref, *refs):
        step = pl.program_id(0)
        left = refs[: 2 * terms]
        right = refs[2 * terms : 2 * terms + terms * len(segments)]
        out_ref, acc_ref = refs[-2:]

        @pl.when(step == 0)
        def _():
            if total is None:
                acc_ref[...] = jnp.zeros_like(acc_ref)
            else:
                acc_ref[...] = refs[-3][...]

        for k, (lo, hi) in enumerate(spans):

            @pl.when(jnp.logical_and(step >= lo, step < hi))
            def _(k=k):
                rows = [r[...] for r in right[k * terms : (k + 1) * terms]]
                rows = rows[0] if terms == 1 else jnp.concatenate(rows, axis=0)
                for i in range(2):
                    cols = [left[2 * t + i][...] for t in range(terms)]
                    cols = cols[0] if terms == 1 else jnp.concatenate(cols, axis=1)
                    acc_ref[i] += jnp.dot(cols, rows, preferred_element_type=F32)

        @pl.when(step == steps - 1)
        def _():
            if not last:
                out_ref[...] = acc_ref[...]
                return
            for i in range(2):
                for h in range(width // HD):
                    part = acc_ref[i, :, h * HD : (h + 1) * HD]
                    if norm:
                        mean = jnp.mean(part * part, axis=-1, keepdims=True)
                        part = part * lax.rsqrt(mean + EPS)
                    out_ref[i, :, h * HD : (h + 1) * HD] = part.astype(BF16)

    return pl.pallas_call(
        body,
        grid_spec=pltpu.PrefetchScalarGridSpec(
            num_scalar_prefetch=1,
            grid=(steps,),
            in_specs=in_specs,
            out_specs=pl.BlockSpec((2, tokens, width), lambda i, idx: (0, 0, 0)),
            scratch_shapes=[pltpu.VMEM((2, tokens, width), F32)],
        ),
        out_shape=jax.ShapeDtypeStruct((2, tokens, width), BF16 if last else F32),
        cost_estimate=pl.CostEstimate(
            flops=4 * tokens * size * terms * steps * width,
            bytes_accessed=4 * tokens * size * terms * steps,
            transcendentals=0,
        ),
        compiler_params=pltpu.CompilerParams(vmem_limit_bytes=52 * 1024 * 1024),
    )(jnp.stack(index).astype(jnp.int32), *arrays)


def project_keys(features, lower, upper, steps):
    tokens = features[0].shape[0]
    size, width, terms = 512, 256, 2
    count = len(steps) // terms
    table = jnp.stack([jnp.stack([jnp.asarray(n, jnp.int32) for n in s]) for s in steps])
    span = count // 4

    def rows_at(column, busy, t):
        def at(i, idx):
            now = jnp.int32(0)
            for g in busy:
                use = jnp.clip(i, g * span, (g + 1) * span - 1)
                spot = idx[(use * terms + t) * 3 + column]
                now = jnp.where(jnp.logical_or(i >= g * span, g == busy[0]), spot, now)
            return (now, 0)

        return at

    def body(idx_ref, *refs):
        step = pl.program_id(0)
        out_ref, acc_ref = refs[-2:]
        left, right = refs[: 2 * terms], refs[2 * terms : -2]

        @pl.when(step == 0)
        def _():
            acc_ref[...] = jnp.zeros_like(acc_ref)

        for g, (low, up) in enumerate(((0, 2), (0, 3), (1, 2), (1, 3))):

            @pl.when(step // span == g)
            def _(low=low, up=up):
                rows = jnp.concatenate(
                    [
                        jnp.concatenate([right[4 * t + low][...], right[4 * t + up][...]], axis=1)
                        for t in range(terms)
                    ],
                    axis=0,
                )
                for i in range(2):
                    cols = jnp.concatenate([left[2 * t + i][...] for t in range(terms)], axis=1)
                    acc_ref[i] += jnp.dot(cols, rows, preferred_element_type=F32)

        @pl.when(step == count - 1)
        def _():
            for i in range(2):
                for h in range(4):
                    part = acc_ref[i, :, h * HD : (h + 1) * HD]
                    mean = jnp.mean(part * part, axis=-1, keepdims=True)
                    out_ref[i, :, h * HD : (h + 1) * HD] = (part * lax.rsqrt(mean + EPS)).astype(BF16)

    arrays, in_specs = [], []
    for t in range(terms):
        arrays += features
        in_specs += [
            pl.BlockSpec((tokens, size), lambda i, idx, t=t: (0, idx[(i * terms + t) * 3]))
        ] * 2
    for t in range(terms):
        arrays += [*lower, *upper]
        for column, busy in ((1, (0, 1)), (1, (2, 3)), (2, (0, 2)), (2, (1, 3))):
            in_specs.append(pl.BlockSpec((size, width), rows_at(column, busy, t)))
    shape = (2, tokens, 2 * width)
    return pl.pallas_call(
        body,
        grid_spec=pltpu.PrefetchScalarGridSpec(
            num_scalar_prefetch=1,
            grid=(count,),
            in_specs=in_specs,
            out_specs=pl.BlockSpec(shape, lambda i, idx: (0, 0, 0)),
            scratch_shapes=[pltpu.VMEM(shape, F32)],
        ),
        out_shape=jax.ShapeDtypeStruct(shape, BF16),
        cost_estimate=pl.CostEstimate(
            flops=8 * tokens * size * terms * count * width,
            bytes_accessed=4 * tokens * size * terms * count,
            transcendentals=0,
        ),
        compiler_params=pltpu.CompilerParams(vmem_limit_bytes=52 * 1024 * 1024),
    )(table.reshape(-1), *arrays)


def slots(core, v):
    one, two = mate(core, v, 0), mate(core, v, 1)
    return (v, one, two, mate(core, two, 0))


def after(value, *others):
    return lax.optimization_barrier((value,) + others)[0]


def per_device(
    hidden, vision, image_ids, tile_counts, q_weight, q_gain, k_weight, v_weight, o_weight
):
    pos = tuple(lax.axis_index(a) for a in AXES)
    yh, z, core, x, yl = pos
    zs, xs = slots(core, z), slots(core, x)
    ys = slots(core, yh * 2 + yl)
    requests = hidden.shape[1]
    order = jnp.arange(requests, dtype=jnp.int32)
    same_image = image_ids[:, None] == image_ids[None, :]
    earlier = order[None, :] < order[:, None]
    occurrence = jnp.sum(jnp.logical_and(same_image, earlier), axis=1)
    slot_of = 2 * image_ids + occurrence
    request_at = jnp.sum(jnp.where(slot_of[None, :] == order[:, None], order[None, :], 0), axis=1)

    def column_half(w, which, width):
        return lax.dynamic_slice_in_dim(w, which * width, width, 1)

    def leaving(one, two):
        zpairs = ((z, two), (one, zs[3]))
        return [
            (h * 4 + zz) * 4 + k for zp in zpairs for h in (yh, 1 - yh) for zz in zp for k in range(4)
        ]

    give = cat(column_half(k_weight, 1 - core, 512), column_half(v_weight, 1 - core, 512))
    got = send(give, CORE)
    places = jnp.stack(leaving(zs[2], zs[1]) + leaving(zs[1], zs[2]))
    rows = jnp.take(hidden, jnp.take(request_at, places), axis=1)
    rows = after(rows.transpose(1, 0, 2).reshape(192, 64), give)
    q_give = jnp.dot(
        rows[:96], column_half(q_weight, 1 - core, 4096), preferred_element_type=F32
    )
    q_got = send(q_give, CORE)
    mine = vision.reshape(800, 8192)
    got = after(got, q_give)
    k_mine, v_mine = column_half(k_weight, core, 512), column_half(v_weight, core, 512)
    k_theirs, v_theirs = got[:512], got[512:]
    a0 = jnp.where(core == yl, k_mine[:, :256], k_theirs[:, :256])
    b0 = cat(k_mine[:, 256:], k_theirs[:, 256:])
    c0 = jnp.where(core == x // 2, v_mine, v_theirs)
    c0 = take_rows(c0, (x % 2) * 256, 256)
    c1 = send(c0, YC)
    a1 = send(a0, Z1)
    b1 = send(after(b0, a0, c0), YC)
    theirs = send(after(mine, b0, a0, c0), CORE)
    q_mine = jnp.dot(
        after(rows, a0, c0)[96:], column_half(q_weight, core, 4096), preferred_element_type=F32
    )
    a01 = cat(a0, after(a1, b0))
    a2 = send(a01, Z2)
    c01 = cat(c0, after(c1, a01))
    c2 = send(c01, Z1)
    a0123 = cat(a01, after(a2, c01))
    a4 = send(a0123, Y1)
    c12 = cat(c1, after(c2, a0123))
    d1 = send(c12, X1)
    c0123 = cat(c01, after(c2, c12))
    c3 = send(c0123, Z2)
    q1 = send(after(q_mine[48:], c0123) + q_got[48:], Z1)
    d12 = cat(c12, after(d1, c0123, theirs))
    d2 = send(d12, X2)
    b01 = cat(b0, after(b1, d12))
    b2 = send(b01, Z1)
    c3 = after(c3, b01)
    e1 = send(c3, X1)
    q2 = q_mine[:48] + q_got[:48] + after(q1, c3)
    q3 = send(q2[24:], YC)
    a01234 = cat(a0123, after(a4, q2))
    a5 = send(a01234, Y2)
    q4 = q2[:24] + after(q3, a01234)
    q5 = send(q4[12:], Z2)
    b0123 = cat(b01, after(b2, q4))
    b3 = send(b0123, Z2)
    q6 = q4[:12] + after(q5, b0123)
    q7 = send(q6, YR)
    features = (mine, theirs)

    def color(h, zz):
        return h * 4 + zz

    def both(zz):
        return [color(yh, zz), color(1 - yh, zz)]

    def quarters(places):
        return [p * 4 + xx for p in places for xx in xs]

    def shared(n, own, one, two):
        return (n, ((own, 0, 1), (one, 0, 1), (two, 0, 1), (two, n, 1)))

    halved = [(v_mine, 0, 1), (v_mine, 1, 1), (v_theirs, 0, 1), (v_theirs, 1, 1)]
    index = [(color(yh, z) * 2 + cc) * 2 + t for cc in (core, 1 - core) for t in range(2)]
    index += quarters([color(1 - yh, z)] + both(zs[1]))
    values = project(
        features,
        [(1, tuple(halved)), shared(3, c12, d1, after(d2, q6))],
        index,
        256,
        last=False,
    )
    q8 = q6 + after(q7, values)
    q9 = send(q8, X1)
    e12 = cat(c3, after(e1, q8))
    e2 = send(e12, X2)
    steps = []
    for ks in ((0, 1), (2, 3)):
        for js in ((0, 1), (2, 3)):
            for k in ks:
                for j in js:
                    h, cc = ys[k] // 2, ys[k] % 2
                    spot = (j % 2) * 4 + jnp.where(h == yh, 0, 2) + jnp.where(cc == core, 0, 1)
                    steps.append((color(h, zs[j]) * 2 + cc, (k % 2) * 4 + j, spot))
    keys = project_keys(features, (a01234, after(a5, e12)), (b0123, b3), steps)
    q10 = q8 + after(q9, keys)
    q11 = send(q10, X2)
    value_heads = project(
        features,
        [shared(4, c3, e1, e2)],
        quarters(both(zs[2]) + both(zs[3])),
        256,
        total=after(values, q10),
    )
    value = q10 + after(q11, value_heads)

    raw = value.reshape(4, STEPS, 32, HD)
    norm = raw * lax.rsqrt(jnp.mean(raw * raw, axis=-1, keepdims=True) + EPS)
    gain = lax.dynamic_slice_in_dim(q_gain.reshape(HEADS, HD), core * 32, 32, 0)
    queries = (norm * gain * HD ** (-0.5)).astype(BF16)
    queries = queries.reshape(2, 2 * STEPS, 4, 8, HD).transpose(0, 2, 1, 3, 4).reshape(2, 4, 48, HD)
    queries = jnp.where(core == 0, queries, queries[::-1])
    limits = lax.dynamic_slice_in_dim(tile_counts, (yh * 4 + z) * 2, 2)
    limits = jnp.where(core == 0, limits, limits[::-1])
    usable = (jnp.arange(800, dtype=jnp.int32) // 200)[None, :] < limits[:, None]

    keys = keys.reshape(2, 800, 4, HD)
    scores = jnp.einsum("ikrd,itkd->ikrt", queries, keys, preferred_element_type=F32)
    scores = jnp.where(usable[:, None, None, :], scores, -jnp.inf)
    peak = jnp.max(scores, axis=-1, keepdims=True)
    expo = jnp.exp(scores - peak)
    total = jnp.sum(expo, axis=-1, keepdims=True)
    probs = (expo / total).astype(BF16)
    weight = (peak + jnp.log(total))[..., 0]
    high = lax.reduce_precision(weight, 8, 7)
    middle = lax.reduce_precision(weight - high, 8, 7)
    low = lax.reduce_precision(weight - high - middle, 8, 7)
    weight = jnp.stack([high, middle, low], axis=2)
    weight = jnp.pad(weight, ((0, 0), (0, 0), (0, 13), (0, HD - 48)))
    value_heads = value_heads.reshape(2, 800, 4, HD)
    part = jnp.einsum("ikrt,itkd->ikrd", probs, value_heads, preferred_element_type=F32)
    part = jnp.concatenate([part, weight], axis=2).astype(BF16)
    part = jnp.where(core == 0, part, part[::-1]).transpose(1, 0, 2, 3)
    got = lax.all_to_all(cat(part, part), ("x", "yl"), 0, 0, tiled=True)
    got = got.astype(F32)
    weight = jnp.sum(got[:, :, 48:51, :48], axis=2)[..., None]
    weight = jnp.exp(weight - jnp.max(weight, axis=0, keepdims=True))
    weight = weight / jnp.sum(weight, axis=0, keepdims=True)
    attention = jnp.sum(got[:, :, :48] * weight, axis=0).astype(BF16)
    there = send(attention, CORE)
    attention = jnp.where((core == 0) == (x < 2), attention, there)
    spread = jnp.broadcast_to(attention[None], (8,) + attention.shape)
    attention = lax.all_to_all(spread, ("yh", "z"), 0, 0, tiled=True)
    attention = attention.reshape(96, 1024)
    terms = jnp.dot(attention, o_weight, preferred_element_type=F32).reshape(32, STEPS, 512)
    terms = jnp.take(terms, slot_of, axis=0).reshape(8, 4, STEPS, 512)
    got = lax.all_to_all(terms, ("x", "yl"), 0, 0, tiled=True)
    return jnp.sum(got, axis=0).transpose(1, 0, 2)


def solution(mesh):
    inner = Mesh(mesh.devices.reshape(SIZES), AXES)
    img, head = ("yh", "z", "c"), ("x", "yl")
    placed = (
        P(None, None, img + head),
        P(img, None, head, None),
        P(),
        P(),
        P(img + head, None),
        P(),
        P(img, None),
        P(img, None),
        P(head, img),
    )
    return jax.shard_map(
        per_device, mesh=inner, in_specs=placed, out_specs=P(None, head, img), check_vma=False
    )
```
